512 devices in a mesh: dp: 16 (over y, x), tensor: 32 (over z, core).
Axes of the slice: x: 4, y: 4, z: 16, core: 2. Of those that a mesh axis runs over, the one named last changes fastest.
Arguments:
- activations: bfloat16 [64, 256, 13824], P('dp', None, 'tensor'), may hold values from -6 to 6
- out_grads: bfloat16 [64, 256, 128], P('dp', None, 'tensor'), may hold values from -0.25 to 0.25
- inverses: float32 [32, 432, 128, 128], P('tensor', 'dp'), may hold values from -1 to 5, as said below
- weights: float32 [32, 432, 128], P('tensor', 'dp'), may hold values from -6 to 6
- removal: int32 [32, 432, 128], P('tensor', 'dp'), may hold values from 0 to 1, as said below
Outputs:
- new_inverses: float32 [32, 432, 128, 128], P('tensor', 'dp')
- pruned: float32 [32, 432, 128], P('tensor', 'dp')
The draws below stay inside these ranges and needn't reach their ends.
Inputs may be any that keep to these rules, and one draw needn't show every extreme that they name: Every block inverses[t, k] is symmetric and positive definite. Every block removal[t, k] holds exactly 16 ones.
All inputs are finite; a program needn't handle non-finite values.
Results may differ from the reference program's by a relative error of at most 0.0038.
Values may be sent and summed in bfloat16 or wider, within the bound.
No kernel may reach another device: no remote copies, remote signals or barrier semaphores. Data moves between devices by JAX's collectives and lax.ppermute only.
A program may use at most 128 MiB of HBM per device.

```python
import math
import jax
import jax.numpy as jnp
from jax import lax

C = 13824
B = 128
REMOVED = 16
RT = 4
SEQ = 256
EXAMPLES = 64
TGROUPS = 32
ROWS = 128
GROUP_BLOCKS = 432


def draw_activations(key, part):
    key = jax.random.fold_in(key, 37)
    key_noise, key_mix, key_dir = jax.random.split(key, 3)
    direction_count = 24
    decay_power = 1.0
    strength = 1.6
    noise_part = 0.6 * jax.random.normal(key_noise, (EXAMPLES, SEQ, C), jnp.float32)
    mixing = jax.random.normal(key_mix, (EXAMPLES, direction_count), jnp.float32)
    directions = jax.random.normal(key_dir, (direction_count, C), jnp.float32)
    shared = jnp.zeros((EXAMPLES, C), jnp.float32)
    for term_index in range(direction_count):
        factor = strength * (term_index + 1.0) ** (-decay_power)
        shared = shared + (factor * mixing[:, term_index])[:, None] * directions[term_index][None, :]
    return jnp.clip(noise_part + shared[:, None, :], -6.0, 6.0).astype(jnp.bfloat16)


def draw_inverses(key, part):
    key = jax.random.fold_in(key, 11)
    key_off, key_diag = jax.random.split(key)
    shape = (TGROUPS, GROUP_BLOCKS, B, B)
    off_part = jax.random.uniform(key_off, shape, jnp.float32, -2.0, 2.0) / B
    off_part = 0.5 * (off_part + jnp.swapaxes(off_part, -1, -2))
    diag_part = 2.2 * jnp.exp(jax.random.uniform(key_diag, (TGROUPS, GROUP_BLOCKS, B), jnp.float32, 0.0, math.log(2.0)))
    identity = jnp.eye(B, dtype=jnp.float32)
    return off_part * (1.0 - identity) + identity * diag_part[..., None]


def draw_removal(key, part):
    key = jax.random.fold_in(key, 23)
    scores = jax.random.randint(key, (TGROUPS, GROUP_BLOCKS, B), 0, 1 << 20, jnp.int32)
    scores = scores * B + jnp.arange(B, dtype=jnp.int32)[None, None, :]
    order = jnp.argsort(scores, axis=-1, stable=True)
    ranks = jnp.argsort(order, axis=-1, stable=True).astype(jnp.int32)
    return (ranks < REMOVED).astype(jnp.int32)


def steps_of(own_key, extent, shards, least, top_value):
    def one(dim, shards_of):
        heights = jax.random.uniform(jax.random.fold_in(jax.random.fold_in(own_key, 6), dim), (shards_of,), jnp.float32, least / len(shards), top_value / len(shards))
        return jnp.repeat(jnp.exp(heights), extent[dim] // shards_of).reshape((-1,) + (1,) * (len(extent) - dim - 1))

    loudness = one(*shards[0])
    for cut in shards[1:]:
        loudness = loudness * one(*cut)
    return loudness


def gaussian(stream_key, dims, spread, limit, cuts=(), kind=jnp.bfloat16):
    values = jax.random.normal(stream_key, dims, jnp.float32) * spread
    if len(cuts) > 0:
        values = steps_of(stream_key, dims, cuts, -0.22, 0.18) * values
    return jnp.clip(values, min=-limit, max=limit).astype(kind)


def setup_inputs(seed: int = 0) -> dict:
    splits = jax.random.split(jax.random.key(seed), 6)
    return {
        "activations": draw_activations(jax.random.fold_in(splits[5], 71), 0),
        "out_grads": gaussian(splits[1], (EXAMPLES, SEQ, ROWS), (2 * SEQ) ** -0.5, 0.25, ((0, 16), (2, 32))),
        "inverses": draw_inverses(jax.random.fold_in(splits[5], 71), 0),
        "weights": gaussian(splits[3], (TGROUPS, GROUP_BLOCKS, B), 1.0, 6.0, ((0, 32), (1, 16)), jnp.float32),
        "removal": draw_removal(jax.random.fold_in(splits[5], 71), 0),
    }


def woodbury_surgeon(inverse, gradients, weights, removal):
    highest = lax.Precision.HIGHEST
    examples = gradients.shape[0]
    width = inverse.shape[-1]
    projected = jnp.einsum('enj,nij->nei', gradients, inverse, precision=highest)
    gram_matrix = jnp.einsum('eni,nfi->nef', gradients, projected, precision=highest)
    gram_matrix = gram_matrix + examples * jnp.eye(examples, dtype=jnp.float32)
    gram_factor = jnp.linalg.cholesky(gram_matrix)
    solution = jax.scipy.linalg.cho_solve((gram_factor, True), projected)
    updated = inverse - jnp.einsum('nei,nej->nij', projected, solution, precision=highest)
    removed = removal.astype(jnp.float32)
    identity = jnp.eye(width, dtype=jnp.float32)
    surgeon_system = removed[:, :, None] * updated * removed[:, None, :] + identity[None] * (1.0 - removed)[:, :, None]
    system_factor = jnp.linalg.cholesky(surgeon_system)
    lifted = jax.scipy.linalg.cho_solve((system_factor, True), (removed * weights)[:, :, None])[:, :, 0]
    moved = jnp.einsum('nij,nj->ni', updated, lifted, precision=highest)
    pruned = (1.0 - removed) * (weights - moved)
    return (updated, pruned)

def reference(activations, out_grads, inverses, weights, removal):
    act_float = activations.astype(jnp.float32)
    row_groups = out_grads.astype(jnp.float32).reshape(EXAMPLES, SEQ, TGROUPS, RT).transpose(2, 0, 1, 3)

    def one_group(items):
        rows_here, inverse, weight_here, removal_here = items
        gradients = jnp.einsum('esr,esc->erc', rows_here, act_float, precision=lax.Precision.HIGHEST).astype(jnp.bfloat16)
        blocks = gradients.reshape(EXAMPLES, GROUP_BLOCKS, B).astype(jnp.float32)
        return woodbury_surgeon(inverse, blocks, weight_here, removal_here)
    new_inverses, pruned = lax.map(one_group, (row_groups, inverses, weights, removal))
    return (new_inverses, pruned)
```

```python
import jax
import jax.numpy as jnp
from jax import lax
from jax.experimental import pallas as pl
from jax.experimental.pallas import tpu as pltpu
from jax.sharding import PartitionSpec as P

REMOVED = 16
F32 = jnp.float32
BF16 = jnp.bfloat16


def halves(x):
    high = x.astype(BF16)
    return high, (x - high.astype(F32)).astype(BF16)


def dot_nn(a, b):
    return lax.dot_general(a, b, (((1,), (0,)), ((), ())), preferred_element_type=F32)


def dot_nt(a, b):
    return lax.dot_general(a, b, (((1,), (1,)), ((), ())), preferred_element_type=F32)


def dot_tn(a, b):
    return lax.dot_general(a, b, (((0,), (0,)), ((), ())), preferred_element_type=F32)


def pick(x, lanes):
    return jnp.take_along_axis(x, lanes, axis=1)


def surgeon_kernel(
    grads_ref, inverse_ref, weights_ref, removal_ref,
    updated_ref, pruned_ref,
    blocks_ref, projected_ref, gram_ref, scale_ref, rows_ref,
):
    nblocks, width = weights_ref.shape
    pieces, examples, piece = grads_ref.shape
    pairs = (nblocks + 1) // 2
    pair_of = [(2 * p, min(2 * p + 1, nblocks - 1)) for p in range(pairs)]

    line = jnp.concatenate([grads_ref[c].astype(F32) for c in range(pieces)], axis=1)
    for b in range(nblocks):
        blocks_ref[b] = line[:, b * width:(b + 1) * width].astype(BF16)

    lane = lax.broadcasted_iota(jnp.int32, (examples, width), 1)
    sub = lax.broadcasted_iota(jnp.int32, (examples, width), 0)
    eye = jnp.where(sub == lane % examples, F32(examples), F32(0.0))
    for p, members in enumerate(pair_of):
        both, wide = [], []
        for half, b in enumerate(members):
            g = blocks_ref[b]
            high, low = halves(inverse_ref[b])
            proj = dot_nn(
                jnp.concatenate([g, g], axis=1), jnp.concatenate([high, low], axis=0)
            )
            projected_ref[p, half * examples:(half + 1) * examples, :] = proj
            both.append(jnp.concatenate([g, g], axis=1))
            wide.append(jnp.concatenate(halves(proj), axis=1))
        full = dot_nt(jnp.concatenate(both, axis=0), jnp.concatenate(wide, axis=0))
        gram_ref[p] = eye + jnp.where(lane < examples, full[:examples], full[examples:])
    scale_ref[...] = jnp.zeros(scale_ref.shape, F32)

    base = (lax.broadcasted_iota(jnp.int32, (8, width), 1) // examples) * examples
    lane8 = lax.broadcasted_iota(jnp.int32, (8, width), 1)
    sub8 = lax.broadcasted_iota(jnp.int32, (8, width), 0)
    for group in range(examples // 8):
        def step(within, carry, group=group):
            k = group * 8 + within
            index = base + k
            own = lane8 == index
            after = sub8 > within
            here = sub8 == within
            rows = [gram_ref[p, pl.ds(k, 1), :] for p in range(pairs)]
            useds, roots = [], []
            for p in range(pairs):
                row = jnp.broadcast_to(rows[p], (8, width))
                root = lax.rsqrt(pick(row, index))
                over = root * root
                scale_ref[p] = jnp.where(own, over, scale_ref[p])
                useds.append(jnp.where(own, F32(0.0), row * over))
                roots.append(root)
            for p in range(pairs):
                used, root = useds[p], roots[p]
                tile = gram_ref[p, group * 8:group * 8 + 8, :]
                factor = jnp.where(after, pick(tile, index), F32(0.0))
                gram_ref[p, group * 8:group * 8 + 8, :] = (
                    jnp.where(here, tile * root, tile) - factor * used
                )
                for v in range(group + 1, examples // 8):
                    tile = gram_ref[p, v * 8:v * 8 + 8, :]
                    gram_ref[p, v * 8:v * 8 + 8, :] = tile - pick(tile, index) * used
            return carry

        lax.fori_loop(0, 8, step, 0)

    removal = removal_ref[...]
    removed = removal.astype(F32)
    a = lax.broadcasted_iota(jnp.int32, (width, width), 0)
    c = lax.broadcasted_iota(jnp.int32, (width, width), 1)
    count = dot_nn(removed.astype(BF16), jnp.where(a <= c, F32(1.0), F32(0.0)).astype(BF16))
    position = jnp.where(removal > 0, count.astype(jnp.int32) - 1, -1)
    slot = lax.broadcasted_iota(jnp.int32, (2 * REMOVED, width), 0)

    strict = sub > lane % examples
    diagonal = sub == lane % examples
    selects = []
    for p, members in enumerate(pair_of):
        over = jnp.broadcast_to(scale_ref[p, 0:1, :], (examples, width))
        lower = gram_ref[p] * jnp.where(strict, -over, jnp.where(diagonal, over, F32(0.0)))
        zero = jnp.zeros((examples, width), F32)
        diag = jnp.concatenate(
            [jnp.where(lane < examples, lower, zero), jnp.where(lane < examples, zero, lower)],
            axis=0,
        )
        lh, ll = halves(diag)
        ph, pm = halves(projected_ref[p])
        z = dot_nn(jnp.concatenate([lh, ll], axis=1), jnp.concatenate([ph, ph], axis=0))
        z = z + dot_nn(lh, pm)
        for half, b in enumerate(members):
            if half == 1 and members[0] == members[1]:
                continue
            zh, zl = halves(z[half * examples:(half + 1) * examples])
            gone = dot_tn(
                jnp.concatenate([zh, zh, zl], axis=0), jnp.concatenate([zh, zl, zh], axis=0)
            )
            new = inverse_ref[b] - gone
            updated_ref[b] = new
            select = jnp.where(slot == position[b:b + 1, :], F32(1.0), F32(0.0))
            selects.append(select.astype(BF16))
            nh, nl = halves(new)
            pick16 = select[:REMOVED].astype(BF16)
            rows_ref[b] = dot_nn(
                jnp.concatenate([pick16, pick16], axis=1), jnp.concatenate([nh, nl], axis=0)
            )

    lane16 = lax.broadcasted_iota(jnp.int32, (REMOVED, width), 1)
    sub16 = lax.broadcasted_iota(jnp.int32, (REMOVED, width), 0)
    base16 = (lane16 // 32) * 32
    systems = []
    for q in range(0, nblocks, 4):
        members = [min(q + j, nblocks - 1) for j in range(4)]
        left = jnp.concatenate(
            [jnp.concatenate(halves(rows_ref[b]), axis=1) for b in members], axis=0
        )
        right = jnp.concatenate([selects[b] for b in members], axis=0)
        full = dot_nt(left, jnp.concatenate([right, right], axis=1))
        system = jnp.zeros((REMOVED, width), F32)
        for j, b in enumerate(members):
            system = jnp.where(base16 == 32 * j, full[REMOVED * j:REMOVED * (j + 1)], system)
            chosen = jnp.sum(
                selects[b][:REMOVED].astype(F32) * weights_ref[b:b + 1, :], axis=1, keepdims=True
            )
            system = jnp.where(lane16 == 32 * j + REMOVED, chosen, system)
        systems.append(system)
    for k in range(REMOVED):
        for i, system in enumerate(systems):
            row = jnp.broadcast_to(system[k:k + 1, :], (REMOVED, width))
            row = row / pick(row, base16 + k)
            factor = pick(system, base16 + k)
            systems[i] = jnp.where(sub16 == k, row, system - factor * row)
    moved = []
    for b in range(nblocks):
        lifted = pick(systems[b // 4], jnp.full((REMOVED, width), 32 * (b % 4) + REMOVED, jnp.int32))
        moved.append(jnp.sum(lifted * rows_ref[b], axis=0, keepdims=True))
    moved = jnp.concatenate(moved, axis=0)
    pruned_ref[...] = (1.0 - removed) * (weights_ref[...] - moved)


def surgeon(grads, inverse, weights, removal):
    nblocks, width = weights.shape
    examples = grads.shape[1]
    pairs = (nblocks + 1) // 2
    vmem = pl.BlockSpec(memory_space=pltpu.VMEM)
    return pl.pallas_call(
        surgeon_kernel,
        out_shape=(
            jax.ShapeDtypeStruct(inverse.shape, F32),
            jax.ShapeDtypeStruct(weights.shape, F32),
        ),
        in_specs=[vmem] * 4,
        out_specs=(vmem, vmem),
        scratch_shapes=[
            pltpu.VMEM((nblocks, examples, width), BF16),
            pltpu.VMEM((pairs, 2 * examples, width), F32),
            pltpu.VMEM((pairs, examples, width), F32),
            pltpu.VMEM((pairs, 8, width), F32),
            pltpu.VMEM((nblocks, REMOVED, width), F32),
        ],
        compiler_params=pltpu.CompilerParams(vmem_limit_bytes=40 * 1024 * 1024),
        name="surgeon",
    )(grads, inverse, weights, removal)


def body(activations, out_grads, inverses, weights, removal):
    examples, tokens, columns = activations.shape
    rows = out_grads.shape[2]
    groups = lax.axis_size("tensor")
    parts = lax.axis_size("dp")
    every_row = lax.all_gather(out_grads, "tensor", axis=2, tiled=True)
    partial_grads = jnp.einsum(
        "esr,esc->erc", every_row, activations, preferred_element_type=F32
    ).astype(BF16)
    sent = partial_grads.reshape(examples, groups, rows, columns).transpose(1, 2, 0, 3)
    mine = lax.all_to_all(sent, "tensor", 0, 0, tiled=True)
    spans = parts // rows
    pieces = groups // spans
    mine = mine.reshape(spans, pieces, rows, examples, columns).transpose(2, 0, 1, 3, 4)
    owned = lax.all_to_all(
        mine.reshape(parts, pieces, examples, columns), "dp", 0, 0, tiled=True
    )
    owned = owned.transpose(1, 0, 2, 3).reshape(pieces, parts * examples, columns)
    updated, pruned = surgeon(owned, inverses[0], weights[0], removal[0])
    return (updated[None], pruned[None])


def solution(mesh):
    placed = (
        P("dp", None, "tensor"),
        P("dp", None, "tensor"),
        P("tensor", "dp", None, None),
        P("tensor", "dp", None),
        P("tensor", "dp", None),
    )
    return jax.shard_map(
        body,
        mesh=mesh,
        in_specs=placed,
        out_specs=(P("tensor", "dp", None, None), P("tensor", "dp", None)),
        check_vma=False,
    )
```

```python
import jax
import jax.numpy as jnp
from jax import lax
from jax.experimental import pallas as pl
from jax.experimental.pallas import tpu as pltpu
from jax.sharding import PartitionSpec as P

REMOVED = 16
CORES = 2
F32 = jnp.float32
BF16 = jnp.bfloat16


def halves(x):
    high = x.astype(BF16)
    return high, (x - high.astype(F32)).astype(BF16)


def dot_nn(a, b):
    return lax.dot_general(a, b, (((1,), (0,)), ((), ())), preferred_element_type=F32)


def dot_nt(a, b):
    return lax.dot_general(a, b, (((1,), (1,)), ((), ())), preferred_element_type=F32)


def dot_tn(a, b):
    return lax.dot_general(a, b, (((0,), (0,)), ((), ())), preferred_element_type=F32)


def pick(x, lanes):
    return jnp.take_along_axis(x, lanes, axis=1)


def surgeon_kernel(
    grads_ref, inverse_ref, weights_ref, removal_ref,
    updated_ref, pruned_ref,
    blocks_ref, projected_ref, gram_ref, scale_ref, rows_ref,
):
    nblocks, width = weights_ref.shape
    pieces, examples, piece = grads_ref.shape
    pairs = (nblocks + 1) // 2
    pair_of = [(2 * p, min(2 * p + 1, nblocks - 1)) for p in range(pairs)]

    line = jnp.concatenate([grads_ref[c].astype(F32) for c in range(pieces)], axis=1)
    for b in range(nblocks):
        blocks_ref[b] = line[:, b * width:(b + 1) * width].astype(BF16)

    lane = lax.broadcasted_iota(jnp.int32, (examples, width), 1)
    sub = lax.broadcasted_iota(jnp.int32, (examples, width), 0)
    eye = jnp.where(sub == lane % examples, F32(examples), F32(0.0))
    for p, members in enumerate(pair_of):
        both, wide = [], []
        for half, b in enumerate(members):
            g = blocks_ref[b]
            high, low = halves(inverse_ref[b])
            proj = dot_nn(
                jnp.concatenate([g, g], axis=1), jnp.concatenate([high, low], axis=0)
            )
            projected_ref[p, half * examples:(half + 1) * examples, :] = proj
            both.append(jnp.concatenate([g, g], axis=1))
            wide.append(jnp.concatenate(halves(proj), axis=1))
        full = dot_nt(jnp.concatenate(both, axis=0), jnp.concatenate(wide, axis=0))
        gram_ref[p] = eye + jnp.where(lane < examples, full[:examples], full[examples:])
    scale_ref[...] = jnp.zeros(scale_ref.shape, F32)

    base = (lax.broadcasted_iota(jnp.int32, (8, width), 1) // examples) * examples
    lane8 = lax.broadcasted_iota(jnp.int32, (8, width), 1)
    sub8 = lax.broadcasted_iota(jnp.int32, (8, width), 0)
    for first in range(0, examples, 8):
        tiles = [gram_ref[p, first:first + 8, :] for p in range(pairs)]
        scales = [scale_ref[p] for p in range(pairs)]
        columns = [[pick(t, base + (first + j)) for j in range(8)] for t in tiles]
        for k in range(8):
            own = lane8 == base + (first + k)
            for p in range(pairs):
                tile, column = tiles[p], columns[p]
                root = lax.rsqrt(jnp.broadcast_to(column[k][k:k + 1, :], (8, width)))
                over = root * root
                scales[p] = jnp.where(own, over, scales[p])
                factor = jnp.where(sub8 > k, column[k], F32(0.0)) * over
                row = jnp.broadcast_to(tile[k:k + 1, :], (8, width))
                used = jnp.where(own, F32(0.0), row)
                tiles[p] = jnp.where(sub8 == k, tile * root, tile) - factor * used
                for j in range(k + 1, 8):
                    column[j] = column[j] - factor * jnp.broadcast_to(
                        column[j][k:k + 1, :], (8, width)
                    )
        rest = first + 8
        for p in range(pairs):
            scale_ref[p] = scales[p]
            gram_ref[p, first:rest, :] = tiles[p]
            if rest == examples:
                continue
            eight = jnp.where(lane8 == base + first + sub8, F32(0.0), tiles[p])
            high = eight.astype(BF16).astype(F32)
            middle = (eight - high).astype(BF16).astype(F32)
            low = eight - high - middle
            full = dot_tn(
                jnp.concatenate([high, high, middle, middle, high, low], axis=0).astype(BF16),
                jnp.concatenate([high, middle, high, middle, low, high], axis=0).astype(BF16),
            )
            gram_ref[p, rest:examples, :] = gram_ref[p, rest:examples, :] - jnp.where(
                lane[rest:] < examples, full[rest:examples], full[examples + rest:]
            )

    removal = removal_ref[...]
    removed = removal.astype(F32)
    a = lax.broadcasted_iota(jnp.int32, (width, width), 0)
    c = lax.broadcasted_iota(jnp.int32, (width, width), 1)
    count = dot_nn(removed.astype(BF16), jnp.where(a <= c, F32(1.0), F32(0.0)).astype(BF16))
    position = jnp.where(removal > 0, count.astype(jnp.int32) - 1, -1)
    slot = lax.broadcasted_iota(jnp.int32, (2 * REMOVED, width), 0)

    strict = sub > lane % examples
    diagonal = sub == lane % examples
    selects = []
    for p, members in enumerate(pair_of):
        over = jnp.broadcast_to(scale_ref[p, 0:1, :], (examples, width))
        lower = gram_ref[p] * jnp.where(strict, -over, jnp.where(diagonal, over, F32(0.0)))
        zero = jnp.zeros((examples, width), F32)
        diag = jnp.concatenate(
            [jnp.where(lane < examples, lower, zero), jnp.where(lane < examples, zero, lower)],
            axis=0,
        )
        lh, ll = halves(diag)
        ph, pm = halves(projected_ref[p])
        z = dot_nn(jnp.concatenate([lh, ll], axis=1), jnp.concatenate([ph, ph], axis=0))
        z = z + dot_nn(lh, pm)
        for half, b in enumerate(members):
            if half == 1 and members[0] == members[1]:
                continue
            zh, zl = halves(z[half * examples:(half + 1) * examples])
            gone = dot_tn(
                jnp.concatenate([zh, zh, zl], axis=0), jnp.concatenate([zh, zl, zh], axis=0)
            )
            new = inverse_ref[b] - gone
            updated_ref[b] = new
            select = jnp.where(slot == position[b:b + 1, :], F32(1.0), F32(0.0))
            selects.append(select.astype(BF16))
            nh, nl = halves(new)
            pick16 = select[:REMOVED].astype(BF16)
            rows_ref[b] = dot_nn(
                jnp.concatenate([pick16, pick16], axis=1), jnp.concatenate([nh, nl], axis=0)
            )

    lane16 = lax.broadcasted_iota(jnp.int32, (REMOVED, width), 1)
    sub16 = lax.broadcasted_iota(jnp.int32, (REMOVED, width), 0)
    base16 = (lane16 // 32) * 32
    systems = []
    for q in range(0, nblocks, 4):
        members = [min(q + j, nblocks - 1) for j in range(4)]
        left = jnp.concatenate(
            [jnp.concatenate(halves(rows_ref[b]), axis=1) for b in members], axis=0
        )
        right = jnp.concatenate([selects[b] for b in members], axis=0)
        full = dot_nt(left, jnp.concatenate([right, right], axis=1))
        system = jnp.zeros((REMOVED, width), F32)
        for j, b in enumerate(members):
            system = jnp.where(base16 == 32 * j, full[REMOVED * j:REMOVED * (j + 1)], system)
            chosen = jnp.sum(
                selects[b][:REMOVED].astype(F32) * weights_ref[b:b + 1, :], axis=1, keepdims=True
            )
            system = jnp.where(lane16 == 32 * j + REMOVED, chosen, system)
        systems.append(system)
    for k in range(REMOVED):
        for i, system in enumerate(systems):
            row = jnp.broadcast_to(system[k:k + 1, :], (REMOVED, width))
            row = row / pick(row, base16 + k)
            factor = pick(system, base16 + k)
            systems[i] = jnp.where(sub16 == k, row, system - factor * row)
    moved = []
    for b in range(nblocks):
        lifted = pick(systems[b // 4], jnp.full((REMOVED, width), 32 * (b % 4) + REMOVED, jnp.int32))
        moved.append(jnp.sum(lifted * rows_ref[b], axis=0, keepdims=True))
    moved = jnp.concatenate(moved, axis=0)
    pruned_ref[...] = (1.0 - removed) * (weights_ref[...] - moved)


def surgeon(grads, inverse, weights, removal):
    nblocks, width = weights.shape
    examples = grads.shape[1]
    pairs = (nblocks + 1) // 2
    vmem = pl.BlockSpec(memory_space=pltpu.VMEM)
    return pl.pallas_call(
        surgeon_kernel,
        out_shape=(
            jax.ShapeDtypeStruct(inverse.shape, F32),
            jax.ShapeDtypeStruct(weights.shape, F32),
        ),
        in_specs=[vmem] * 4,
        out_specs=(vmem, vmem),
        scratch_shapes=[
            pltpu.VMEM((nblocks, examples, width), BF16),
            pltpu.VMEM((pairs, 2 * examples, width), F32),
            pltpu.VMEM((pairs, examples, width), F32),
            pltpu.VMEM((pairs, 8, width), F32),
            pltpu.VMEM((nblocks, REMOVED, width), F32),
        ],
        compiler_params=pltpu.CompilerParams(vmem_limit_bytes=40 * 1024 * 1024),
        name="surgeon",
    )(grads, inverse, weights, removal)


def body(activations, out_grads, inverses, weights, removal):
    examples, tokens, columns = activations.shape
    rows = out_grads.shape[2]
    groups = lax.axis_size("tensor")
    parts = lax.axis_size("dp")
    chips = groups // CORES
    same_core = [[chip * CORES + core for chip in range(chips)] for core in range(CORES)]
    core = lax.axis_index("tensor") % CORES
    other = lax.ppermute(activations, "tensor", [(t, t ^ 1) for t in range(groups)])
    every = lax.all_to_all(
        jnp.broadcast_to(out_grads.transpose(2, 0, 1)[None], (chips, rows, examples, tokens)),
        "tensor", 0, 0, axis_index_groups=same_core, tiled=True,
    ).reshape(chips * rows, examples, tokens)
    here, there = (
        jnp.einsum("res,esc->erc", every, a, preferred_element_type=F32).astype(BF16)
        for a in (activations, other)
    )
    partial_grads = jnp.concatenate(
        [jnp.where(core == 0, here, there), jnp.where(core == 0, there, here)], axis=2
    )
    columns = CORES * columns
    sent = partial_grads.reshape(examples, chips, rows, columns).transpose(1, 2, 0, 3)
    mine = lax.all_to_all(sent, "tensor", 0, 0, axis_index_groups=same_core, tiled=True)
    spans = parts // rows
    pieces = chips // spans
    mine = mine.reshape(spans, pieces, rows, examples, columns).transpose(2, 0, 1, 3, 4)
    owned = lax.all_to_all(
        mine.reshape(parts, pieces, examples, columns), "dp", 0, 0, tiled=True
    )
    owned = owned.transpose(1, 0, 2, 3).reshape(pieces, parts * examples, columns)
    updated, pruned = surgeon(owned, inverses[0], weights[0], removal[0])
    return (updated[None], pruned[None])


def solution(mesh):
    placed = (
        P("dp", None, "tensor"),
        P("dp", None, "tensor"),
        P("tensor", "dp", None, None),
        P("tensor", "dp", None),
        P("tensor", "dp", None),
    )
    return jax.shard_map(
        body,
        mesh=mesh,
        in_specs=placed,
        out_specs=(P("tensor", "dp", None, None), P("tensor", "dp", None)),
        check_vma=False,
    )
```
